128 devices in a mesh: node: 32 (over y, z, core), head: 4 (over x).
Axes of the slice: x: 4, y: 4, z: 4, core: 2. Of those that a mesh axis runs over, the one named last changes fastest.
Arguments:
- queries: bfloat16 [8192, 5120], P(('node', 'head')), may hold values from -100 to 100
- keys: bfloat16 [8192, 1024], P(('node', 'head')), may hold values from -6 to 6
- values: bfloat16 [8192, 1024], P(('node', 'head')), may hold values from -6 to 6
- out_grad: bfloat16 [8192, 5120], P(('node', 'head')), may hold values from -6 to 6
- parent: int32 [32], replicated, may hold values from -1 to 7, as said below
- node_of_slot: int32 [32], replicated, may hold values from 0 to 31, each once
- live_tiles: int32 [32], replicated, may hold values from 1 to 2, as said below
Outputs:
- attended: bfloat16 [8192, 5120], P(('node', 'head'))
- query_grad: bfloat16 [8192, 5120], P(('node', 'head'))
- key_grad: bfloat16 [8192, 1024], P(('node', 'head'))
- value_grad: bfloat16 [8192, 1024], P(('node', 'head'))
The draws below stay inside these ranges and needn't reach their ends.
Inputs may be any that keep to these rules, and one draw needn't show every extreme that they name: Node 0 is the root with parent -1; every other node's parent has a smaller index and is below 8, so only nodes 0 to 7 have children; a path from the root holds at most four nodes. `live_tiles`: the root's segment is full.
All inputs are finite; a program needn't handle non-finite values.
Results may differ from the reference program's by a relative error of at most 0.0085.
Values may be sent and summed in bfloat16 or wider, within the bound.
No kernel may reach another device: no remote copies, remote signals or barrier semaphores. Data moves between devices by JAX's collectives and lax.ppermute only.
A program may use at most 128 MiB of HBM per device.

```python
import jax
import jax.numpy as jnp
from jax import lax

HQ = 40
HK = 8
HD = 128
SEG = 256
TILE = 128
TILES = 2
NODES = 32
TOKENS = 8192


def shared_keys(key):
    return jnp.clip(jax.random.normal(key, (TOKENS, HK * HD), jnp.float32), -6.0, 6.0)


def draw_keys(key, part):
    base = shared_keys(key)
    return base.astype(jnp.bfloat16)


def draw_queries(key, part):
    key = jax.random.fold_in(key, 2)
    noise = jax.random.normal(key, (TOKENS, HQ * HD), jnp.float32)
    noise = jnp.clip(noise, -6.0, 6.0)
    return noise.astype(jnp.bfloat16)


def draw_parent(key, part):
    key = jax.random.fold_in(key, 3)
    first, second = jax.random.split(key)
    inner = NODES // 4
    top = max(1, (inner - 1) // 2)
    index = jnp.arange(NODES)
    middle = jax.random.randint(first, (NODES,), 1, top + 1)
    leaves = jax.random.randint(second, (NODES,), 0, inner)
    leaves = jnp.where(index == NODES - 1, inner - 1, leaves)
    chosen = jnp.where(index <= top, 0, jnp.where(index < inner, middle, leaves))
    return jnp.where(index == 0, -1, chosen).astype(jnp.int32)


def draw_live_tiles(key, part):
    key = jax.random.fold_in(key, 4)
    counts = jax.random.randint(key, (NODES,), 1, TILES + 1)
    return jnp.where(jnp.arange(NODES) == 0, TILES, counts).astype(jnp.int32)


def levels(rng, dims, shards, least, high):
    factor_of = 1.0
    for dim, parts in shards:
        heights = jax.random.uniform(jax.random.fold_in(jax.random.fold_in(rng, 6), dim), (parts,), jnp.float32, least / len(shards), high / len(shards))
        factor_of = factor_of * jnp.repeat(jnp.exp(heights), dims[dim] // parts).reshape((-1,) + (1,) * (len(dims) - 1 - dim))
    return factor_of


def bell_draw(stream_key, extent, width, most, cuts=(), held_as=jnp.bfloat16):
    factor_of = levels(stream_key, extent, cuts, -0.22, 0.18) if cuts else 1.0
    entries = jax.random.normal(stream_key, extent, jnp.float32) * width * factor_of
    return jnp.minimum(jnp.maximum(entries, -most), most).astype(held_as)


def setup_inputs(seed: int = 0) -> dict:
    splits = jax.random.split(jax.random.key(seed), 8)
    queries = draw_queries(jax.random.fold_in(splits[7], 71), 0)
    keys = draw_keys(jax.random.fold_in(splits[7], 71), 0)
    values = bell_draw(splits[2], (TOKENS, HK * HD), 1.0, 6.0, ((0, 128),))
    out_grad = bell_draw(splits[3], (TOKENS, HQ * HD), 1.0, 6.0, ((0, 128),))
    parent = draw_parent(jax.random.fold_in(splits[7], 71), 0)
    node_of_slot = jax.random.permutation(splits[5], NODES).astype(jnp.int32)
    live_tiles = draw_live_tiles(jax.random.fold_in(splits[7], 71), 0)
    return {"queries": queries, "keys": keys, "values": values, "out_grad": out_grad, "parent": parent, "node_of_slot": node_of_slot, "live_tiles": live_tiles}


def lineage(start_node, parent):
    chain = [start_node]
    current = start_node
    for _ in range(3):
        upper = jnp.where(current >= 0, parent[jnp.maximum(current, 0)], -1)
        chain.append(upper)
        current = upper
    return jnp.stack(chain).astype(jnp.int32)


def build_mask(valid, live, seg_len, tile_len):
    rows = jnp.arange(seg_len)[:, None]
    columns = jnp.arange(4 * seg_len)[None, :]
    block = columns // seg_len
    position = columns % seg_len
    own = (block == 0) & (position <= rows)
    far = (block > 0) & valid[block] & (position // tile_len < live[block])
    return own | far


def local_pass(query_rows, grad_rows, blocks, allowed, head_size):
    seg_len = query_rows.shape[0]
    kv_width = blocks.shape[2] // 2
    kv_heads = kv_width // head_size
    group_size = query_rows.shape[1] // kv_width
    scale = head_size ** -0.5
    flat = blocks.reshape(4 * seg_len, 2 * kv_width).astype(jnp.float32)
    key_rows = flat[:, :kv_width].reshape(4 * seg_len, kv_heads, head_size)
    value_rows = flat[:, kv_width:].reshape(4 * seg_len, kv_heads, head_size)
    query_four = query_rows.astype(jnp.float32).reshape(seg_len, kv_heads, group_size, head_size)
    grad_four = grad_rows.astype(jnp.float32).reshape(seg_len, kv_heads, group_size, head_size)
    scores = jnp.einsum('rkgd,tkd->kgrt', query_four, key_rows) * scale
    masked = jnp.where(allowed, scores, -jnp.inf)
    peak = jnp.max(masked, axis=-1, keepdims=True)
    total = jnp.sum(jnp.exp(masked - peak), axis=-1, keepdims=True)
    probs = jnp.exp(masked - (peak + jnp.log(total)))
    probs_b = probs.astype(jnp.bfloat16).astype(jnp.float32)
    attended = jnp.einsum('kgrt,tkd->rkgd', probs_b, value_rows).astype(jnp.bfloat16)
    delta = jnp.einsum('rkgd,rkgd->kgr', grad_four, attended.astype(jnp.float32))
    dprobs = jnp.einsum('rkgd,tkd->kgrt', grad_four, value_rows)
    dscores = (probs * (dprobs - delta[..., None])).astype(jnp.bfloat16).astype(jnp.float32)
    query_grad = (scale * jnp.einsum('kgrt,tkd->rkgd', dscores, key_rows)).astype(jnp.bfloat16)
    key_terms = jnp.einsum('kgrt,rkgd->tkd', dscores, query_four).reshape(4 * seg_len, kv_width)
    value_terms = jnp.einsum('kgrt,rkgd->tkd', probs_b, grad_four).reshape(4 * seg_len, kv_width)
    terms = jnp.concatenate([key_terms, value_terms], 1).reshape(4, seg_len, 2 * kv_width)
    return attended.reshape(seg_len, -1), query_grad.reshape(seg_len, -1), terms


def reference(queries, keys, values, out_grad, parent, node_of_slot, live_tiles):
    node_ids = jnp.arange(NODES, dtype=jnp.int32)
    slot_of_node = jnp.sum(node_ids[None, :] * (node_of_slot[None, :] == node_ids[:, None]), axis=1).astype(jnp.int32)
    kv_width = HK * HD
    paired = jnp.concatenate([keys, values], 1).reshape(NODES, SEG, 2 * kv_width)
    query_seg = queries.reshape(NODES, SEG, HQ * HD)
    grad_seg = out_grad.reshape(NODES, SEG, HQ * HD)

    def per_slot(slot):
        chain = lineage(node_of_slot[slot], parent)
        valid = chain >= 0
        safe = jnp.maximum(chain, 0)
        slots = jnp.where(valid, slot_of_node[safe], 0).astype(jnp.int32)
        live = jnp.where(valid, live_tiles[safe], 0)
        allowed = build_mask(valid, live, SEG, TILE)
        attended, query_grad, terms = local_pass(query_seg[slot], grad_seg[slot], paired[slots], allowed, HD)
        terms = terms * valid.astype(jnp.float32)[:, None, None]
        return attended, query_grad, terms, slots

    attended, query_grad, terms, slots = lax.map(per_slot, jnp.arange(NODES, dtype=jnp.int32))
    sums = jnp.zeros((NODES, SEG, 2 * kv_width), jnp.float32).at[slots.reshape(-1)].add(terms.reshape(-1, SEG, 2 * kv_width))
    sums = sums.reshape(TOKENS, 2 * kv_width)
    key_grad = (HD ** -0.5 * sums[:, :kv_width]).astype(jnp.bfloat16)
    value_grad = sums[:, kv_width:].astype(jnp.bfloat16)
    return attended.reshape(TOKENS, -1), query_grad.reshape(TOKENS, -1), key_grad, value_grad
```

```python
import functools

import jax
import jax.numpy as jnp
from jax import lax
from jax.experimental import pallas as pl
from jax.experimental.pallas import tpu as pltpu
from jax.sharding import Mesh
from jax.sharding import PartitionSpec as P

HD = 128
TILE = 128
SEG = 256
GROUP = 5
KV_HEADS = 8
INNER = 8
NODES = 32
CHIPS = 16
QW = GROUP * HD
WIDE = 2 * QW + 2 * HD
SCALE = HD ** (-0.5)
BF = jnp.bfloat16
F32 = jnp.float32

ALL = ("chip", "core", "head")
GROUP_AXES = ("core", "head")


def smem():
    return pl.BlockSpec(memory_space=pltpu.SMEM)


def vmem():
    return pl.BlockSpec(memory_space=pltpu.VMEM)


def nt_dot(left, right):
    return lax.dot_general(left, right, (((1,), (1,)), ((), ())), preferred_element_type=F32)


def nn_dot(left, right):
    return lax.dot_general(left, right, (((1,), (0,)), ((), ())), preferred_element_type=F32)


def select_kernel(node_of_slot, pieces, out):
    for slot in range(NODES):
        node = node_of_slot[slot]

        @pl.when(node < INNER)
        def _():
            row = pl.multiple_of(node * 32, 32)
            block = pieces[slot]
            for chip in range(CHIPS):
                out[chip, pl.ds(row, 32), :] = block


def attention_kernel(
    chip, parent, node_of_slot, live_tiles, mine, far, out, terms, key_all, value_all, bias, acc
):
    acc[...] = jnp.zeros_like(acc)

    def per_slot(core, carry):
        base = pl.multiple_of(core * SEG, SEG)
        me = node_of_slot[2 * chip[0] + core]
        key_all[0:SEG, :] = mine[pl.ds(base, SEG), 2 * QW : 2 * QW + HD]
        value_all[0:SEG, :] = mine[pl.ds(base, SEG), 2 * QW + HD : WIDE]
        token = lax.broadcasted_iota(jnp.int32, (SEG, SEG), 0)
        row = lax.broadcasted_iota(jnp.int32, (SEG, SEG), 1)
        bias[0:SEG, :] = jnp.where(token <= row, 0.0, -jnp.inf)
        tile = lax.rem(token, 32) // 16
        current = me
        starts = []
        for step in range(1, 4):
            upper = jnp.where(current >= 0, parent[jnp.maximum(current, 0)], -1)
            safe = jnp.maximum(upper, 0)
            live = jnp.where(upper >= 0, live_tiles[safe], 0)
            start = pl.multiple_of(safe * 32, 32)
            starts.append(start)
            here = slice(step * SEG, (step + 1) * SEG)
            key_all[here, :] = far[0:8, pl.ds(start, 32), :].reshape(SEG, HD)
            value_all[here, :] = far[8:16, pl.ds(start, 32), :].reshape(SEG, HD)
            bias[here, :] = jnp.where(tile < live, 0.0, -jnp.inf)
            current = upper

        keys = key_all[...]
        values = value_all[...]
        keys_t = keys.T
        values_t = values.T
        key_terms = jnp.zeros((4 * SEG, HD), F32)
        value_terms = jnp.zeros((4 * SEG, HD), F32)
        for g in range(GROUP):
            columns = slice(g * HD, (g + 1) * HD)
            grad_columns = slice(QW + g * HD, QW + (g + 1) * HD)
            query = mine[pl.ds(base, SEG), columns]
            grad = mine[pl.ds(base, SEG), grad_columns]
            scores = nt_dot(keys, query) * SCALE + bias[...]
            peak = jnp.max(scores, axis=0, keepdims=True)
            weight = jnp.exp(scores - peak)
            total = jnp.sum(weight, axis=0, keepdims=True)
            probs = weight * (1.0 / total)
            probs_b = probs.astype(BF)
            attended = nn_dot(values_t, probs_b).T.astype(BF)
            out[pl.ds(base, SEG), columns] = attended
            delta = jnp.sum(
                grad.astype(F32).T * attended.astype(F32).T, axis=0, keepdims=True
            )
            dprobs = nt_dot(values, grad)
            dscores = (probs * (dprobs - delta)).astype(BF)
            query_grad = nn_dot(keys_t, dscores) * SCALE
            out[pl.ds(base, SEG), grad_columns] = query_grad.T.astype(BF)
            key_terms = key_terms + nn_dot(dscores, query)
            value_terms = value_terms + nn_dot(probs_b, grad)
        key_terms = key_terms * SCALE
        out[pl.ds(base, SEG), 2 * QW : 2 * QW + HD] = key_terms[0:SEG].astype(BF)
        out[pl.ds(base, SEG), 2 * QW + HD : WIDE] = value_terms[0:SEG].astype(BF)
        for step in range(1, 4):
            start = starts[step - 1]
            here = slice(step * SEG, (step + 1) * SEG)
            acc[0:8, pl.ds(start, 32), :] += key_terms[here].reshape(8, 32, HD)
            acc[8:16, pl.ds(start, 32), :] += value_terms[here].reshape(8, 32, HD)

        @pl.when(me < INNER)
        def _():
            for piece in range(8):
                for quarter in range(4):
                    first = quarter * 64 + piece * 8
                    where = pl.ds(pl.multiple_of(me * 32 + quarter * 8, 8), 8)
                    acc[piece, where, :] += key_terms[first : first + 8]
                    acc[8 + piece, where, :] += value_terms[first : first + 8]

        return carry

    lax.fori_loop(0, 2, per_slot, 0)
    terms[...] = acc[...].astype(BF)


def sum_kernel(node_of_slot, parts, out, total):
    sums = parts[0].astype(F32)
    for chip in range(1, CHIPS):
        sums = sums + parts[chip].astype(F32)
    total[...] = sums.astype(BF)
    for slot in range(NODES):
        node = node_of_slot[slot]

        @pl.when(node < INNER)
        def _():
            out[slot] = total[pl.ds(pl.multiple_of(node * 32, 32), 32), :]

        @pl.when(node >= INNER)
        def _():
            out[slot] = jnp.zeros((32, HD), BF)


def on_device(queries, keys, values, out_grad, parent, node_of_slot, live_tiles):
    rows = queries.shape[0]
    chip = lax.axis_index("chip")
    core = lax.axis_index("core")

    pieces = jnp.concatenate([keys, values], 0).reshape(16, 8, KV_HEADS, HD)
    pieces = pieces.transpose(0, 2, 1, 3).reshape(CHIPS * KV_HEADS, 8, HD)
    pieces = lax.all_to_all(pieces, ALL, split_axis=0, concat_axis=0, tiled=True)
    inner = pl.pallas_call(
        select_kernel,
        out_shape=jax.ShapeDtypeStruct((CHIPS, INNER * 32, HD), BF),
        in_specs=[smem(), vmem()],
        out_specs=vmem(),
        name="select_inner",
    )(node_of_slot, pieces.reshape(NODES, 32, HD))
    far = lax.all_to_all(inner, "chip", split_axis=0, concat_axis=0, tiled=True)

    def by_head(array, width):
        return array.reshape(rows, KV_HEADS, width).transpose(1, 0, 2)

    mine = jnp.concatenate(
        [by_head(queries, QW), by_head(out_grad, QW), by_head(keys, HD), by_head(values, HD)], 2
    )
    mine = lax.all_to_all(mine, GROUP_AXES, split_axis=0, concat_axis=0, tiled=True)

    out, terms = pl.pallas_call(
        attention_kernel,
        out_shape=(
            jax.ShapeDtypeStruct((2 * SEG, WIDE), BF),
            jax.ShapeDtypeStruct((CHIPS, INNER * 32, HD), BF),
        ),
        in_specs=[smem(), smem(), smem(), smem(), vmem(), vmem()],
        out_specs=(vmem(), vmem()),
        scratch_shapes=[
            pltpu.VMEM((4 * SEG, HD), BF),
            pltpu.VMEM((4 * SEG, HD), BF),
            pltpu.VMEM((4 * SEG, SEG), F32),
            pltpu.VMEM((CHIPS, INNER * 32, HD), F32),
        ],
        compiler_params=pltpu.CompilerParams(vmem_limit_bytes=48 * 1024 * 1024),
        cost_estimate=pl.CostEstimate(
            flops=2 * 5 * 10 * SEG * 4 * SEG * HD,
            bytes_accessed=6 * 1024 * 1024,
            transcendentals=10 * SEG * 4 * SEG,
        ),
        name="attention",
    )(chip[None], parent, node_of_slot, live_tiles, mine.reshape(2 * SEG, WIDE), far)

    parts = lax.all_to_all(terms, "chip", split_axis=0, concat_axis=0, tiled=True)
    sums = pl.pallas_call(
        sum_kernel,
        out_shape=jax.ShapeDtypeStruct((NODES, 32, HD), BF),
        in_specs=[smem(), vmem()],
        out_specs=vmem(),
        scratch_shapes=[pltpu.VMEM((INNER * 32, HD), BF)],
        name="sum_terms",
    )(node_of_slot, parts)
    sums = sums.reshape(CHIPS * KV_HEADS, 8, HD)
    sums = lax.all_to_all(sums, ALL, split_axis=0, concat_axis=0, tiled=True)
    sums = sums.reshape(2, 8, KV_HEADS, 8, HD).transpose(0, 1, 3, 2, 4)
    sums = sums.reshape(2, rows, KV_HEADS * HD)

    back = lax.all_to_all(
        out.reshape(KV_HEADS, rows, WIDE), GROUP_AXES, split_axis=0, concat_axis=0, tiled=True
    )
    back = back.transpose(1, 0, 2)
    attended = back[:, :, :QW].reshape(rows, KV_HEADS * QW)
    query_grad = back[:, :, QW : 2 * QW].reshape(rows, KV_HEADS * QW)
    own_key = back[:, :, 2 * QW : 2 * QW + HD].reshape(rows, KV_HEADS * HD)
    own_value = back[:, :, 2 * QW + HD :].reshape(rows, KV_HEADS * HD)
    is_inner = node_of_slot[2 * chip + core] < INNER
    key_grad = jnp.where(is_inner, sums[0], own_key)
    value_grad = jnp.where(is_inner, sums[1], own_value)
    return attended, query_grad, key_grad, value_grad


def solution(mesh):
    devices = mesh.devices.reshape(CHIPS, 2, 4)
    inner_mesh = Mesh(devices, ALL)
    split = P(ALL, None)
    return jax.shard_map(
        on_device,
        mesh=inner_mesh,
        in_specs=(split, split, split, split, P(), P(), P()),
        out_specs=(split, split, split, split),
        check_vma=False,
    )
```

```python
import functools

import jax
import jax.numpy as jnp
from jax import lax
from jax.experimental import pallas as pl
from jax.experimental.pallas import tpu as pltpu
from jax.sharding import Mesh
from jax.sharding import PartitionSpec as P

HD = 128
TILE = 128
SEG = 256
GROUP = 5
KV_HEADS = 8
INNER = 8
NODES = 32
CHIPS = 16
QW = GROUP * HD
WIDE = 2 * QW + 2 * HD
SCALE = HD ** (-0.5)
BF = jnp.bfloat16
F32 = jnp.float32
MIB = 1024 * 1024
LOG2_E = 1.4426950408889634

PARENT, NODE_OF_SLOT, LIVE_TILES, PLACE = 0, 32, 64, 96

ALL = ("chip", "core", "head")
GROUP_AXES = ("core", "head")


def smem():
    return pl.BlockSpec(memory_space=pltpu.SMEM)


def vmem():
    return pl.BlockSpec(memory_space=pltpu.VMEM)


def nt_dot(left, right):
    return lax.dot_general(left, right, (((1,), (1,)), ((), ())), preferred_element_type=F32)


def nn_dot(left, right):
    return lax.dot_general(left, right, (((1,), (0,)), ((), ())), preferred_element_type=F32)


def select_kernel(info, pieces, out):
    for slot in range(NODES):
        node = info[NODE_OF_SLOT + slot]

        @pl.when(node < INNER)
        def _():
            row = pl.multiple_of(node * 32, 32)
            block = pieces[slot]
            for chip in range(CHIPS):
                out[chip, pl.ds(row, 32), :] = block


SHIFTS = (0, 2, 1, 3)
PIECES = [(dc, dx) for dc in range(2) for dx in SHIFTS]


def group_index(info, dc, dx):
    return lax.rem(info[PLACE + 1] + dc, 2) * 4 + lax.rem(info[PLACE + 2] + dx, 4)


def pack_kernel(info, queries, out_grad, keys, values, *outs):
    for (dc, dx), out in zip(PIECES, outs):
        peer = group_index(info, dc, dx)
        wide = pl.ds(pl.multiple_of(peer * QW, HD), QW)
        narrow = pl.ds(pl.multiple_of(peer * HD, HD), HD)
        out[:, 0:QW] = queries[:, wide]
        out[:, QW : 2 * QW] = out_grad[:, wide]
        out[:, 2 * QW : 2 * QW + HD] = keys[:, narrow]
        out[:, 2 * QW + HD : WIDE] = values[:, narrow]


def unpack_kernel(info, *refs):
    pieces, (attended, query_grad, own_key, own_value) = refs[:8], refs[8:]
    for (dc, dx), piece in zip(PIECES, pieces):
        peer = group_index(info, 2 - dc, 4 - dx)
        wide = pl.ds(pl.multiple_of(peer * QW, HD), QW)
        narrow = pl.ds(pl.multiple_of(peer * HD, HD), HD)
        attended[:, wide] = piece[:, 0:QW]
        query_grad[:, wide] = piece[:, QW : 2 * QW]
        own_key[:, narrow] = piece[:, 2 * QW : 2 * QW + HD]
        own_value[:, narrow] = piece[:, 2 * QW + HD : WIDE]


def exchange(pieces, shifts):
    moved = []
    for (dc, dx), piece in zip(shifts, pieces):
        if dc or dx:
            pairs = [
                (4 * c + x, 4 * ((c + dc) % 2) + (x + dx) % 4) for c in range(2) for x in range(4)
            ]
            piece = lax.ppermute(piece, GROUP_AXES, pairs)
        moved.append(piece)
    return moved


def copy_all(sources, targets, sems):
    copies = [
        pltpu.make_async_copy(source, target, sems.at[n])
        for n, (source, target) in enumerate(zip(sources, targets))
    ]
    for copy in copies:
        copy.start()
    return copies


def attention_kernel(dc, info, far, *refs):
    arrived, refs = refs[:4], refs[4:]
    if dc == 0:
        leaving, key_out, value_out, refs = refs[:4], refs[4], refs[5], refs[6:]
    else:
        first_key, first_value, leaving, terms, refs = refs[0], refs[1], refs[2:6], refs[6], refs[7:]
    mine, out, key_all, value_all, bias, probs_all, dscores_all, sems = refs[:8]
    quarters = [
        pl.ds(pl.multiple_of(lax.rem(info[PLACE + 2] + 4 - dx, 4) * 64, 64), 64) for dx in SHIFTS
    ]
    copies = copy_all(arrived, [mine.at[quarter, :] for quarter in quarters], sems)
    row = lax.broadcasted_iota(jnp.int32, (SEG, SEG), 0)
    token = lax.broadcasted_iota(jnp.int32, (SEG, SEG), 1)
    bias[:, 0:SEG] = jnp.where(token <= row, 0.0, -jnp.inf)
    tile = lax.rem(token, 32) // 16

    def lineage(which):
        me = info[NODE_OF_SLOT + 2 * info[PLACE] + lax.rem(info[PLACE + 1] + which, 2)]
        chain = [me]
        for _ in range(3):
            current = chain[-1]
            chain.append(jnp.where(current >= 0, info[PARENT + jnp.maximum(current, 0)], -1))
        return chain

    for step, node in enumerate(lineage(dc)[1:], 1):
        safe = jnp.maximum(node, 0)
        live = jnp.where(node >= 0, info[LIVE_TILES + safe], 0)
        rows = pl.ds(pl.multiple_of(safe * 32, 32), 32)
        here = slice(step * SEG, (step + 1) * SEG)
        key_all[here, :] = far[0:8, rows, :].reshape(SEG, HD)
        value_all[here, :] = far[8:16, rows, :].reshape(SEG, HD)
        bias[:, here] = jnp.where(tile < live, 0.0, -jnp.inf)
    for copy in copies:
        copy.wait()
    key_all[0:SEG, :] = mine[:, 2 * QW : 2 * QW + HD]
    value_all[0:SEG, :] = mine[:, 2 * QW + HD : WIDE]

    keys = key_all[...]
    values = value_all[...]
    queries_t = []
    grads_t = []
    for g in range(GROUP):
        columns = slice(g * HD, (g + 1) * HD)
        grad_columns = slice(QW + g * HD, QW + (g + 1) * HD)
        query = mine[:, columns]
        grad = mine[:, grad_columns]
        queries_t.append(query.T)
        grads_t.append(grad.T)
        scores = nt_dot(query, keys) * (SCALE * LOG2_E) + bias[...]
        peak = jnp.max(scores, axis=1, keepdims=True)
        weight = jnp.exp2(scores - peak)
        total = jnp.sum(weight, axis=1, keepdims=True)
        probs = weight * (1.0 / total)
        probs_b = probs.astype(BF)
        attended = nn_dot(probs_b, values).astype(BF)
        out[:, columns] = attended
        delta = jnp.sum(grad.astype(F32) * attended.astype(F32), axis=1, keepdims=True)
        dprobs = nt_dot(grad, values)
        dscores = (probs * (dprobs - delta)).astype(BF)
        query_grad = nn_dot(dscores, keys) * SCALE
        out[:, grad_columns] = query_grad.astype(BF)
        probs_all[g * SEG : (g + 1) * SEG, :] = probs_b
        dscores_all[g * SEG : (g + 1) * SEG, :] = dscores
    key_terms = nn_dot(jnp.concatenate(queries_t, 1), dscores_all[...]).T * SCALE
    value_terms = nn_dot(jnp.concatenate(grads_t, 1), probs_all[...]).T
    out[:, 2 * QW : 2 * QW + HD] = key_terms[0:SEG].astype(BF)
    out[:, 2 * QW + HD : WIDE] = value_terms[0:SEG].astype(BF)
    quarters = [
        pl.ds(pl.multiple_of(lax.rem(info[PLACE + 2] + dx, 4) * 64, 64), 64) for dx in SHIFTS
    ]
    copies = copy_all([out.at[quarter, :] for quarter in quarters], leaving, sems)

    if dc == 0:
        key_out[...] = key_terms
        value_out[...] = value_terms
    else:
        acc = refs[8]
        acc[...] = jnp.zeros_like(acc)
        for chain, key_part, value_part in (
            (lineage(0), first_key, first_value),
            (lineage(1), key_terms, value_terms),
        ):
            for step in range(1, 4):
                rows = pl.ds(pl.multiple_of(jnp.maximum(chain[step], 0) * 32, 32), 32)
                here = slice(step * SEG, (step + 1) * SEG)
                acc[0:8, rows, :] += key_part[here].reshape(8, 32, HD)
                acc[8:16, rows, :] += value_part[here].reshape(8, 32, HD)

            @pl.when(chain[0] < INNER)
            def _():
                for piece in range(8):
                    for quarter in range(4):
                        first = quarter * 64 + piece * 8
                        rows = pl.ds(pl.multiple_of(chain[0] * 32 + quarter * 8, 8), 8)
                        acc[piece, rows, :] += key_part[first : first + 8]
                        acc[8 + piece, rows, :] += value_part[first : first + 8]

        terms[...] = acc[...].astype(BF)
    for copy in copies:
        copy.wait()


def sum_kernel(info, parts, out, total):
    sums = parts[0].astype(F32)
    for chip in range(1, CHIPS):
        sums = sums + parts[chip].astype(F32)
    total[...] = sums.astype(BF)
    for slot in range(NODES):
        node = info[NODE_OF_SLOT + slot]

        @pl.when(node < INNER)
        def _():
            out[slot] = total[pl.ds(pl.multiple_of(node * 32, 32), 32), :]

        @pl.when(node >= INNER)
        def _():
            out[slot] = jnp.zeros((32, HD), BF)


def on_device(queries, keys, values, out_grad, parent, node_of_slot, live_tiles):
    rows = queries.shape[0]
    chip = lax.axis_index("chip")
    core = lax.axis_index("core")
    place = jnp.stack([chip, core, lax.axis_index("head"), 0]).astype(jnp.int32)
    info = jnp.concatenate([parent, node_of_slot, live_tiles, place])

    pieces = jnp.concatenate([keys, values], 0).reshape(16, 8, KV_HEADS, HD)
    pieces = pieces.transpose(0, 2, 1, 3).reshape(CHIPS * KV_HEADS, 8, HD)
    pieces = lax.all_to_all(pieces, ALL, split_axis=0, concat_axis=0, tiled=True)
    piece_shape = jax.ShapeDtypeStruct((rows, WIDE), BF)
    packed = pl.pallas_call(
        pack_kernel,
        out_shape=(piece_shape,) * 8,
        in_specs=[smem()] + [vmem()] * 4,
        out_specs=(vmem(),) * 8,
        compiler_params=pltpu.CompilerParams(vmem_limit_bytes=8 * MIB),
        name="pack",
    )(info, queries, out_grad, keys, values)
    pieces, packed = lax.optimization_barrier((pieces, packed))
    inner = pl.pallas_call(
        select_kernel,
        out_shape=jax.ShapeDtypeStruct((CHIPS, INNER * 32, HD), BF),
        in_specs=[smem(), vmem()],
        out_specs=vmem(),
        compiler_params=pltpu.CompilerParams(vmem_limit_bytes=6 * MIB),
        name="select_inner",
    )(info, pieces.reshape(NODES, 32, HD))
    far = lax.all_to_all(inner, "chip", split_axis=0, concat_axis=0, tiled=True)
    arrived = exchange(packed, PIECES)

    any_memory = pl.BlockSpec(memory_space=pl.ANY)
    half = jax.ShapeDtypeStruct((4 * SEG, HD), F32)

    def attend(dc, operands):
        last = dc == 1
        out_shape = (piece_shape,) * 4
        out_specs = (any_memory,) * 4
        scratch_shapes = [
            pltpu.VMEM((SEG, WIDE), BF),
            pltpu.VMEM((SEG, WIDE), BF),
            pltpu.VMEM((4 * SEG, HD), BF),
            pltpu.VMEM((4 * SEG, HD), BF),
            pltpu.VMEM((SEG, 4 * SEG), F32),
            pltpu.VMEM((GROUP * SEG, 4 * SEG), BF),
            pltpu.VMEM((GROUP * SEG, 4 * SEG), BF),
            pltpu.SemaphoreType.DMA((4,)),
        ]
        if last:
            out_shape += (jax.ShapeDtypeStruct((CHIPS, INNER * 32, HD), BF),)
            out_specs += (vmem(),)
            scratch_shapes.append(pltpu.VMEM((CHIPS, INNER * 32, HD), F32))
        else:
            out_shape += (half, half)
            out_specs += (vmem(), vmem())
        return pl.pallas_call(
            functools.partial(attention_kernel, dc),
            out_shape=out_shape,
            in_specs=[smem(), vmem()] + [any_memory] * 4 + [vmem()] * (2 if last else 0),
            out_specs=out_specs,
            scratch_shapes=scratch_shapes,
            compiler_params=pltpu.CompilerParams(vmem_limit_bytes=28 * MIB),
            cost_estimate=pl.CostEstimate(
                flops=2 * 5 * GROUP * SEG * 4 * SEG * HD * 4,
                bytes_accessed=6 * 1024 * 1024,
                transcendentals=GROUP * SEG * 4 * SEG,
            ),
            name="attention",
        )(info, far, *operands)

    *leaving, first_key, first_value = attend(0, arrived[:4])
    *others, terms = attend(1, arrived[4:] + [first_key, first_value])
    first_back = exchange(leaving, PIECES[:4])
    terms, first_back = lax.optimization_barrier((terms, first_back))

    parts = lax.all_to_all(terms, "chip", split_axis=0, concat_axis=0, tiled=True)
    back = first_back + exchange(others, PIECES[4:])
    parts, back = lax.optimization_barrier((parts, back))
    sums = pl.pallas_call(
        sum_kernel,
        out_shape=jax.ShapeDtypeStruct((NODES, 32, HD), BF),
        in_specs=[smem(), vmem()],
        out_specs=vmem(),
        scratch_shapes=[pltpu.VMEM((INNER * 32, HD), BF)],
        compiler_params=pltpu.CompilerParams(vmem_limit_bytes=6 * MIB),
        name="sum_terms",
    )(info, parts)
    sums = sums.reshape(CHIPS * KV_HEADS, 8, HD)
    sums = lax.all_to_all(sums, ALL, split_axis=0, concat_axis=0, tiled=True)

    wide_shape = jax.ShapeDtypeStruct((rows, KV_HEADS * QW), BF)
    narrow_shape = jax.ShapeDtypeStruct((rows, KV_HEADS * HD), BF)
    attended, query_grad, own_key, own_value = pl.pallas_call(
        unpack_kernel,
        out_shape=(wide_shape, wide_shape, narrow_shape, narrow_shape),
        in_specs=[smem()] + [vmem()] * 8,
        out_specs=(vmem(),) * 4,
        compiler_params=pltpu.CompilerParams(vmem_limit_bytes=8 * MIB),
        name="unpack",
    )(info, *back)
    sums, attended, query_grad, own_key, own_value = lax.optimization_barrier(
        (sums, attended, query_grad, own_key, own_value)
    )
    sums = sums.reshape(2, 8, KV_HEADS, 8, HD).transpose(0, 1, 3, 2, 4)
    sums = sums.reshape(2, rows, KV_HEADS * HD)
    is_inner = node_of_slot[2 * chip + core] < INNER
    key_grad = jnp.where(is_inner, sums[0], own_key)
    value_grad = jnp.where(is_inner, sums[1], own_value)
    return attended, query_grad, key_grad, value_grad


def solution(mesh):
    devices = mesh.devices.reshape(CHIPS, 2, 4)
    inner_mesh = Mesh(devices, ALL)
    split = P(ALL, None)
    return jax.shard_map(
        on_device,
        mesh=inner_mesh,
        in_specs=(split, split, split, split, P(), P(), P()),
        out_specs=(split, split, split, split),
        check_vma=False,
    )
```

```python
import functools

import jax
import jax.numpy as jnp
from jax import lax
from jax.experimental import pallas as pl
from jax.experimental.pallas import tpu as pltpu
from jax.sharding import Mesh
from jax.sharding import PartitionSpec as P

HD = 128
TILE = 128
SEG = 256
GROUP = 5
KV_HEADS = 8
INNER = 8
NODES = 32
CHIPS = 16
QW = GROUP * HD
WIDE = 2 * QW + 2 * HD
SCALE = HD ** (-0.5)
BF = jnp.bfloat16
F32 = jnp.float32
MIB = 1024 * 1024
LOG2_E = 1.4426950408889634

PARENT, NODE_OF_SLOT, LIVE_TILES, SLOT_OF_NODE, PLACE = 0, 32, 64, 96, 128
INFO_SIZE = 131

ALL = ("chip", "core", "head")
GROUP_AXES = ("core", "head")


def smem():
    return pl.BlockSpec(memory_space=pltpu.SMEM)


def vmem():
    return pl.BlockSpec(memory_space=pltpu.VMEM)


def hbm():
    return pl.BlockSpec(memory_space=pltpu.HBM)


def nt_dot(left, right):
    return lax.dot_general(left, right, (((1,), (1,)), ((), ())), preferred_element_type=F32)


def nn_dot(left, right):
    return lax.dot_general(left, right, (((1,), (0,)), ((), ())), preferred_element_type=F32)


def info_kernel(parent, node_of_slot, live_tiles, info):
    for n in range(NODES):
        info[PARENT + n] = parent[n]
        info[NODE_OF_SLOT + n] = node_of_slot[n]
        info[LIVE_TILES + n] = live_tiles[n]
    for slot in range(NODES):
        info[SLOT_OF_NODE + node_of_slot[slot]] = slot
    for n, axis in enumerate(ALL):
        info[PLACE + n] = lax.axis_index(axis)


def select_kernel(info, pieces, out):
    for node in range(INNER):
        block = pieces[info[SLOT_OF_NODE + node]]
        for chip in range(CHIPS):
            out[chip, node * 32 : node * 32 + 32, :] = block


SHIFTS = (0, 2, 1, 3)
PIECES = [(dc, dx) for dc in range(2) for dx in SHIFTS]


def group_index(info, dc, dx):
    return lax.rem(info[PLACE + 1] + dc, 2) * 4 + lax.rem(info[PLACE + 2] + dx, 4)


def pack_kernel(info, queries, out_grad, keys, values, *outs):
    for (dc, dx), out in zip(PIECES, outs):
        peer = group_index(info, dc, dx)
        wide = pl.ds(pl.multiple_of(peer * QW, HD), QW)
        narrow = pl.ds(pl.multiple_of(peer * HD, HD), HD)
        out[:, 0:QW] = queries[:, wide]
        out[:, QW : 2 * QW] = out_grad[:, wide]
        out[:, 2 * QW : 2 * QW + HD] = keys[:, narrow]
        out[:, 2 * QW + HD : WIDE] = values[:, narrow]


def unpack_kernel(info, *refs):
    pieces, (attended, query_grad, own_key, own_value) = refs[:8], refs[8:]
    for (dc, dx), piece in zip(PIECES, pieces):
        peer = group_index(info, 2 - dc, 4 - dx)
        wide = pl.ds(pl.multiple_of(peer * QW, HD), QW)
        narrow = pl.ds(pl.multiple_of(peer * HD, HD), HD)
        attended[:, wide] = piece[:, 0:QW]
        query_grad[:, wide] = piece[:, QW : 2 * QW]
        own_key[:, narrow] = piece[:, 2 * QW : 2 * QW + HD]
        own_value[:, narrow] = piece[:, 2 * QW + HD : WIDE]


def exchange(pieces, shifts):
    moved = []
    for (dc, dx), piece in zip(shifts, pieces):
        if dc or dx:
            pairs = [
                (4 * c + x, 4 * ((c + dc) % 2) + (x + dx) % 4) for c in range(2) for x in range(4)
            ]
            piece = lax.ppermute(piece, GROUP_AXES, pairs)
        moved.append(piece)
    return moved


def attention_kernel(dc, info, far, *refs):
    arrived, refs = refs[:4], refs[4:]
    if dc == 0:
        leaving, key_out, value_out, refs = refs[:4], refs[4], refs[5], refs[6:]
    else:
        first_key, first_value, leaving, terms, refs = refs[0], refs[1], refs[2:6], refs[6], refs[7:]
    mine, out, key_all, value_all, bias, probs_all, dscores_all = refs[:7]
    sems = refs[7]
    quarters = [
        pl.ds(pl.multiple_of(lax.rem(info[PLACE + 2] + 4 - dx, 4) * 64, 64), 64) for dx in SHIFTS
    ]
    copies = []
    for n, (quarter, piece) in enumerate(zip(quarters, arrived)):
        if dc == 0:
            copies.append(pltpu.make_async_copy(piece, mine.at[quarter, :], sems.at[n]))
            copies[-1].start()
        else:
            mine[quarter, :] = piece[...]
    row = lax.broadcasted_iota(jnp.int32, (SEG, SEG), 0)
    token = lax.broadcasted_iota(jnp.int32, (SEG, SEG), 1)
    bias[:, 0:SEG] = jnp.where(token <= row, 0.0, -jnp.inf)
    tile = (token >> 4) & 1

    def lineage(which):
        me = info[NODE_OF_SLOT + 2 * info[PLACE] + lax.rem(info[PLACE + 1] + which, 2)]
        chain = [me]
        for _ in range(3):
            current = chain[-1]
            chain.append(jnp.where(current >= 0, info[PARENT + jnp.maximum(current, 0)], -1))
        return chain

    def accumulate(chain, key_part, value_part):
        for step in range(1, 4):
            rows = pl.ds(pl.multiple_of(jnp.maximum(chain[step], 0) * 32, 32), 32)
            here = slice(step * SEG, (step + 1) * SEG)
            acc[0:8, rows, :] += key_part[here].reshape(8, 32, HD)
            acc[8:16, rows, :] += value_part[here].reshape(8, 32, HD)

        @pl.when(chain[0] < INNER)
        def _():
            for piece in range(8):
                for quarter in range(4):
                    first = quarter * 64 + piece * 8
                    rows = pl.ds(pl.multiple_of(chain[0] * 32 + quarter * 8, 8), 8)
                    acc[piece, rows, :] += key_part[first : first + 8]
                    acc[8 + piece, rows, :] += value_part[first : first + 8]

    if dc == 1:
        acc = refs[8]
        acc[...] = jnp.zeros_like(acc)
        accumulate(lineage(0), first_key, first_value)

    for step, node in enumerate(lineage(dc)[1:], 1):
        safe = jnp.maximum(node, 0)
        live = jnp.where(node >= 0, info[LIVE_TILES + safe], 0)
        rows = pl.ds(pl.multiple_of(safe * 32, 32), 32)
        here = slice(step * SEG, (step + 1) * SEG)
        key_all[here, :] = far[0:8, rows, :].reshape(SEG, HD)
        value_all[here, :] = far[8:16, rows, :].reshape(SEG, HD)
        bias[:, here] = jnp.where(tile < live, 0.0, -jnp.inf)
    for copy in copies:
        copy.wait()
    key_all[0:SEG, :] = mine[:, 2 * QW : 2 * QW + HD]
    value_all[0:SEG, :] = mine[:, 2 * QW + HD : WIDE]

    keys = key_all[...]
    values = value_all[...]
    queries_t = []
    grads_t = []
    for g in range(GROUP):
        columns = slice(g * HD, (g + 1) * HD)
        grad_columns = slice(QW + g * HD, QW + (g + 1) * HD)
        query = mine[:, columns]
        grad = mine[:, grad_columns]
        queries_t.append(query.T)
        grads_t.append(grad.T)
        scores = nt_dot(query, keys) * (SCALE * LOG2_E) + bias[...]
        peak = jnp.max(scores, axis=1, keepdims=True)
        weight = jnp.exp2(scores - peak)
        total = jnp.sum(weight, axis=1, keepdims=True)
        probs = weight * (1.0 / total)
        probs_b = probs.astype(BF)
        attended = nn_dot(probs_b, values).astype(BF)
        out[:, columns] = attended
        delta = jnp.sum(grad.astype(F32) * attended.astype(F32), axis=1, keepdims=True)
        dprobs = nt_dot(grad, values)
        dscores = (probs * (dprobs - delta)).astype(BF)
        query_grad = nn_dot(dscores, keys) * SCALE
        out[:, grad_columns] = query_grad.astype(BF)
        probs_all[g * SEG : (g + 1) * SEG, :] = probs_b
        dscores_all[g * SEG : (g + 1) * SEG, :] = dscores
    key_terms = nn_dot(jnp.concatenate(queries_t, 1), dscores_all[...]).T * SCALE
    value_terms = nn_dot(jnp.concatenate(grads_t, 1), probs_all[...]).T
    out[:, 2 * QW : 2 * QW + HD] = key_terms[0:SEG].astype(BF)
    out[:, 2 * QW + HD : WIDE] = value_terms[0:SEG].astype(BF)
    quarters = [
        pl.ds(pl.multiple_of(lax.rem(info[PLACE + 2] + dx, 4) * 64, 64), 64) for dx in SHIFTS
    ]
    for quarter, piece in zip(quarters, leaving):
        piece[...] = out[quarter, :]

    if dc == 0:
        key_out[...] = key_terms
        value_out[...] = value_terms
    else:
        accumulate(lineage(1), key_terms, value_terms)
        terms[...] = acc[...].astype(BF)


def sum_kernel(info, parts, out):
    out[...] = jnp.zeros_like(out)
    for node in range(INNER):
        rows = slice(node * 32, node * 32 + 32)
        sums = parts[0, rows, :].astype(F32)
        for chip in range(1, CHIPS):
            sums = sums + parts[chip, rows, :].astype(F32)
        out[info[SLOT_OF_NODE + node]] = sums.astype(BF)


def on_device(queries, keys, values, out_grad, parent, node_of_slot, live_tiles):
    rows = queries.shape[0]
    chip = lax.axis_index("chip")
    core = lax.axis_index("core")
    info = pl.pallas_call(
        info_kernel,
        out_shape=pltpu.SMEM((INFO_SIZE,), jnp.int32),
        in_specs=[smem()] * 3,
        out_specs=smem(),
        name="info",
    )(parent, node_of_slot, live_tiles)

    pieces = jnp.concatenate([keys, values], 0).reshape(16, 8, KV_HEADS, HD)
    pieces = pieces.transpose(0, 2, 1, 3).reshape(CHIPS * KV_HEADS, 8, HD)
    pieces = lax.all_to_all(pieces, ALL, split_axis=0, concat_axis=0, tiled=True)
    piece_shape = jax.ShapeDtypeStruct((rows, WIDE), BF)
    packed = pl.pallas_call(
        pack_kernel,
        out_shape=(pltpu.HBM((rows, WIDE), BF),) * 8,
        in_specs=[smem()] + [vmem()] * 4,
        out_specs=(vmem(),) * 8,
        compiler_params=pltpu.CompilerParams(vmem_limit_bytes=8 * MIB),
        name="pack",
    )(info, queries, out_grad, keys, values)
    pieces, packed = lax.optimization_barrier((pieces, packed))
    inner = pl.pallas_call(
        select_kernel,
        out_shape=jax.ShapeDtypeStruct((CHIPS, INNER * 32, HD), BF),
        in_specs=[smem(), vmem()],
        out_specs=vmem(),
        compiler_params=pltpu.CompilerParams(vmem_limit_bytes=6 * MIB),
        name="select_inner",
    )(info, pieces.reshape(NODES, 32, HD))
    far = lax.all_to_all(inner, "chip", split_axis=0, concat_axis=0, tiled=True)
    arrived = exchange(packed, PIECES)
    arrived[:4] = [pltpu.with_memory_space_constraint(piece, pltpu.HBM) for piece in arrived[:4]]

    half = jax.ShapeDtypeStruct((4 * SEG, HD), F32)

    def attend(dc, operands):
        last = dc == 1
        out_shape = (piece_shape,) * 4
        out_specs = (vmem(),) * 4
        scratch_shapes = [
            pltpu.VMEM((SEG, WIDE), BF),
            pltpu.VMEM((SEG, WIDE), BF),
            pltpu.VMEM((4 * SEG, HD), BF),
            pltpu.VMEM((4 * SEG, HD), BF),
            pltpu.VMEM((SEG, 4 * SEG), F32),
            pltpu.VMEM((GROUP * SEG, 4 * SEG), BF),
            pltpu.VMEM((GROUP * SEG, 4 * SEG), BF),
            pltpu.SemaphoreType.DMA((4,)),
        ]
        if last:
            out_shape += (jax.ShapeDtypeStruct((CHIPS, INNER * 32, HD), BF),)
            out_specs += (vmem(),)
            scratch_shapes.append(pltpu.VMEM((CHIPS, INNER * 32, HD), F32))
        else:
            out_shape += (half, half)
            out_specs += (vmem(), vmem())
        return pl.pallas_call(
            functools.partial(attention_kernel, dc),
            out_shape=out_shape,
            in_specs=[smem(), vmem()] + ([vmem()] * 6 if last else [hbm()] * 4),
            out_specs=out_specs,
            scratch_shapes=scratch_shapes,
            compiler_params=pltpu.CompilerParams(vmem_limit_bytes=20 * MIB),
            cost_estimate=pl.CostEstimate(
                flops=2 * 5 * GROUP * SEG * 4 * SEG * HD * 4,
                bytes_accessed=6 * 1024 * 1024,
                transcendentals=GROUP * SEG * 4 * SEG,
            ),
            name="attention",
        )(info, far, *operands)

    *leaving, first_key, first_value = attend(0, arrived[:4])
    *others, terms = attend(1, arrived[4:] + [first_key, first_value])
    first_back = exchange(leaving, PIECES[:4])
    terms, first_back = lax.optimization_barrier((terms, first_back))

    parts = lax.all_to_all(terms, "chip", split_axis=0, concat_axis=0, tiled=True)
    back = first_back + exchange(others, PIECES[4:])
    parts, back = lax.optimization_barrier((parts, back))
    sums = pl.pallas_call(
        sum_kernel,
        out_shape=jax.ShapeDtypeStruct((NODES, 32, HD), BF),
        in_specs=[smem(), vmem()],
        out_specs=vmem(),
        compiler_params=pltpu.CompilerParams(vmem_limit_bytes=6 * MIB),
        name="sum_terms",
    )(info, parts)
    sums = sums.reshape(CHIPS * KV_HEADS, 8, HD)
    sums = lax.all_to_all(sums, ALL, split_axis=0, concat_axis=0, tiled=True)

    wide_shape = jax.ShapeDtypeStruct((rows, KV_HEADS * QW), BF)
    narrow_shape = jax.ShapeDtypeStruct((rows, KV_HEADS * HD), BF)
    attended, query_grad, own_key, own_value = pl.pallas_call(
        unpack_kernel,
        out_shape=(wide_shape, wide_shape, narrow_shape, narrow_shape),
        in_specs=[smem()] + [vmem()] * 8,
        out_specs=(vmem(),) * 4,
        compiler_params=pltpu.CompilerParams(vmem_limit_bytes=8 * MIB),
        name="unpack",
    )(info, *back)
    sums, attended, query_grad, own_key, own_value = lax.optimization_barrier(
        (sums, attended, query_grad, own_key, own_value)
    )
    sums = sums.reshape(2, 8, KV_HEADS, 8, HD).transpose(0, 1, 3, 2, 4)
    sums = sums.reshape(2, rows, KV_HEADS * HD)
    is_inner = node_of_slot[2 * chip + core] < INNER
    key_grad = jnp.where(is_inner, sums[0], own_key)
    value_grad = jnp.where(is_inner, sums[1], own_value)
    return attended, query_grad, key_grad, value_grad


def solution(mesh):
    devices = mesh.devices.reshape(CHIPS, 2, 4)
    inner_mesh = Mesh(devices, ALL)
    split = P(ALL, None)
    return jax.shard_map(
        on_device,
        mesh=inner_mesh,
        in_specs=(split, split, split, split, P(), P(), P()),
        out_specs=(split, split, split, split),
        check_vma=False,
    )
```

```python
import functools

import jax
import jax.numpy as jnp
from jax import lax
from jax.experimental import pallas as pl
from jax.experimental.pallas import tpu as pltpu
from jax.sharding import Mesh
from jax.sharding import PartitionSpec as P

HD = 128
TILE = 128
SEG = 256
GROUP = 5
KV_HEADS = 8
INNER = 8
NODES = 32
CHIPS = 16
QW = GROUP * HD
WIDE = 2 * QW + 2 * HD
SCALE = HD ** (-0.5)
BF = jnp.bfloat16
F32 = jnp.float32
MIB = 1024 * 1024
LOG2_E = 1.4426950408889634

PARENT, NODE_OF_SLOT, LIVE_TILES, SLOT_OF_NODE, PLACE = 0, 32, 64, 96, 128
INFO_SIZE = 131

ALL = ("chip", "core", "head")
GROUP_AXES = ("core", "head")


def smem():
    return pl.BlockSpec(memory_space=pltpu.SMEM)


def vmem():
    return pl.BlockSpec(memory_space=pltpu.VMEM)


def hbm():
    return pl.BlockSpec(memory_space=pltpu.HBM)


def nt_dot(left, right):
    return lax.dot_general(left, right, (((1,), (1,)), ((), ())), preferred_element_type=F32)


def nn_dot(left, right):
    return lax.dot_general(left, right, (((1,), (0,)), ((), ())), preferred_element_type=F32)


def info_kernel(parent, node_of_slot, live_tiles, info):
    for n in range(NODES):
        info[PARENT + n] = parent[n]
        info[NODE_OF_SLOT + n] = node_of_slot[n]
        info[LIVE_TILES + n] = live_tiles[n]
    for slot in range(NODES):
        info[SLOT_OF_NODE + node_of_slot[slot]] = slot
    for n, axis in enumerate(ALL):
        info[PLACE + n] = lax.axis_index(axis)


def select_kernel(info, pieces, out):
    for node in range(INNER):
        block = pieces[info[SLOT_OF_NODE + node]]
        for chip in range(CHIPS):
            out[chip, node * 32 : node * 32 + 32, :] = block


SHIFTS = (0, 2, 1, 3)
PIECES = [(dc, dx) for dc in range(2) for dx in SHIFTS]


def group_index(info, dc, dx):
    return lax.rem(info[PLACE + 1] + dc, 2) * 4 + lax.rem(info[PLACE + 2] + dx, 4)


def pack_kernel(info, queries, out_grad, keys, values, *outs):
    for (dc, dx), out in zip(PIECES, outs):
        peer = group_index(info, dc, dx)
        wide = pl.ds(pl.multiple_of(peer * QW, HD), QW)
        narrow = pl.ds(pl.multiple_of(peer * HD, HD), HD)
        out[:, 0:QW] = queries[:, wide]
        out[:, QW : 2 * QW] = out_grad[:, wide]
        out[:, 2 * QW : 2 * QW + HD] = keys[:, narrow]
        out[:, 2 * QW + HD : WIDE] = values[:, narrow]


def unpack_kernel(info, *refs):
    pieces, (attended, query_grad, own_key, own_value) = refs[:8], refs[8:]
    for (dc, dx), piece in zip(PIECES, pieces):
        peer = group_index(info, 2 - dc, 4 - dx)
        wide = pl.ds(pl.multiple_of(peer * QW, HD), QW)
        narrow = pl.ds(pl.multiple_of(peer * HD, HD), HD)
        attended[:, wide] = piece[:, 0:QW]
        query_grad[:, wide] = piece[:, QW : 2 * QW]
        own_key[:, narrow] = piece[:, 2 * QW : 2 * QW + HD]
        own_value[:, narrow] = piece[:, 2 * QW + HD : WIDE]


def exchange(pieces, shifts):
    moved = []
    for (dc, dx), piece in zip(shifts, pieces):
        if dc or dx:
            pairs = [
                (4 * c + x, 4 * ((c + dc) % 2) + (x + dx) % 4) for c in range(2) for x in range(4)
            ]
            piece = lax.ppermute(piece, GROUP_AXES, pairs)
        moved.append(piece)
    return moved


def attention_kernel(dc, info, far, *refs):
    arrived, refs = refs[:4], refs[4:]
    if dc == 0:
        leaving, key_out, value_out, refs = refs[:4], refs[4], refs[5], refs[6:]
    else:
        first_key, first_value, leaving, terms, refs = refs[0], refs[1], refs[2:6], refs[6], refs[7:]
    mine, out, key_all, value_all, bias, probs_all, dscores_all = refs[:7]
    quarters = [
        pl.ds(pl.multiple_of(lax.rem(info[PLACE + 2] + 4 - dx, 4) * 64, 64), 64) for dx in SHIFTS
    ]
    for quarter, piece in zip(quarters, arrived):
        mine[quarter, :] = piece[...]
    row = lax.broadcasted_iota(jnp.int32, (SEG, SEG), 0)
    token = lax.broadcasted_iota(jnp.int32, (SEG, SEG), 1)
    bias[:, 0:SEG] = jnp.where(token <= row, 0.0, -jnp.inf)
    tile = (token >> 4) & 1

    def lineage(which):
        me = info[NODE_OF_SLOT + 2 * info[PLACE] + lax.rem(info[PLACE + 1] + which, 2)]
        chain = [me]
        for _ in range(3):
            current = chain[-1]
            chain.append(jnp.where(current >= 0, info[PARENT + jnp.maximum(current, 0)], -1))
        return chain

    def accumulate(chain, key_part, value_part):
        for step in range(1, 4):
            rows = pl.ds(pl.multiple_of(jnp.maximum(chain[step], 0) * 32, 32), 32)
            here = slice(step * SEG, (step + 1) * SEG)
            acc[0:8, rows, :] += key_part[here].reshape(8, 32, HD)
            acc[8:16, rows, :] += value_part[here].reshape(8, 32, HD)

        @pl.when(chain[0] < INNER)
        def _():
            for piece in range(8):
                for quarter in range(4):
                    first = quarter * 64 + piece * 8
                    rows = pl.ds(pl.multiple_of(chain[0] * 32 + quarter * 8, 8), 8)
                    acc[piece, rows, :] += key_part[first : first + 8]
                    acc[8 + piece, rows, :] += value_part[first : first + 8]

    if dc == 1:
        acc = refs[7]
        acc[...] = jnp.zeros_like(acc)
        accumulate(lineage(0), first_key, first_value)

    for step, node in enumerate(lineage(dc)[1:], 1):
        safe = jnp.maximum(node, 0)
        live = jnp.where(node >= 0, info[LIVE_TILES + safe], 0)
        rows = pl.ds(pl.multiple_of(safe * 32, 32), 32)
        here = slice(step * SEG, (step + 1) * SEG)
        key_all[here, :] = far[0:8, rows, :].reshape(SEG, HD)
        value_all[here, :] = far[8:16, rows, :].reshape(SEG, HD)
        bias[:, here] = jnp.where(tile < live, 0.0, -jnp.inf)
    key_all[0:SEG, :] = mine[:, 2 * QW : 2 * QW + HD]
    value_all[0:SEG, :] = mine[:, 2 * QW + HD : WIDE]

    keys = key_all[...]
    values = value_all[...]
    queries_t = []
    grads_t = []
    for g in range(GROUP):
        columns = slice(g * HD, (g + 1) * HD)
        grad_columns = slice(QW + g * HD, QW + (g + 1) * HD)
        query = mine[:, columns]
        grad = mine[:, grad_columns]
        queries_t.append(query.T)
        grads_t.append(grad.T)
        scores = nt_dot(query, keys) * (SCALE * LOG2_E) + bias[...]
        peak = jnp.max(scores, axis=1, keepdims=True)
        weight = jnp.exp2(scores - peak)
        total = jnp.sum(weight, axis=1, keepdims=True)
        probs = weight * (1.0 / total)
        probs_b = probs.astype(BF)
        attended = nn_dot(probs_b, values).astype(BF)
        out[:, columns] = attended
        delta = jnp.sum(grad.astype(F32) * attended.astype(F32), axis=1, keepdims=True)
        dprobs = nt_dot(grad, values)
        dscores = (probs * (dprobs - delta)).astype(BF)
        query_grad = nn_dot(dscores, keys) * SCALE
        out[:, grad_columns] = query_grad.astype(BF)
        probs_all[g * SEG : (g + 1) * SEG, :] = probs_b
        dscores_all[g * SEG : (g + 1) * SEG, :] = dscores
    key_terms = nn_dot(jnp.concatenate(queries_t, 1), dscores_all[...]).T * SCALE
    value_terms = nn_dot(jnp.concatenate(grads_t, 1), probs_all[...]).T
    out[:, 2 * QW : 2 * QW + HD] = key_terms[0:SEG].astype(BF)
    out[:, 2 * QW + HD : WIDE] = value_terms[0:SEG].astype(BF)
    quarters = [
        pl.ds(pl.multiple_of(lax.rem(info[PLACE + 2] + dx, 4) * 64, 64), 64) for dx in SHIFTS
    ]
    for quarter, piece in zip(quarters, leaving):
        piece[...] = out[quarter, :]

    if dc == 0:
        key_out[...] = key_terms
        value_out[...] = value_terms
    else:
        accumulate(lineage(1), key_terms, value_terms)
        terms[...] = acc[...].astype(BF)


def sum_kernel(info, parts, out):
    out[...] = jnp.zeros_like(out)
    for node in range(INNER):
        rows = slice(node * 32, node * 32 + 32)
        sums = parts[0, rows, :].astype(F32)
        for chip in range(1, CHIPS):
            sums = sums + parts[chip, rows, :].astype(F32)
        out[info[SLOT_OF_NODE + node]] = sums.astype(BF)


def on_device(queries, keys, values, out_grad, parent, node_of_slot, live_tiles):
    rows = queries.shape[0]
    chip = lax.axis_index("chip")
    core = lax.axis_index("core")
    info = pl.pallas_call(
        info_kernel,
        out_shape=pltpu.SMEM((INFO_SIZE,), jnp.int32),
        in_specs=[smem()] * 3,
        out_specs=smem(),
        name="info",
    )(parent, node_of_slot, live_tiles)

    pieces = jnp.concatenate([keys, values], 0).reshape(16, 8, KV_HEADS, HD)
    pieces = pieces.transpose(0, 2, 1, 3).reshape(CHIPS * KV_HEADS, 8, HD)
    pieces = lax.all_to_all(pieces, ALL, split_axis=0, concat_axis=0, tiled=True)
    piece_shape = jax.ShapeDtypeStruct((rows, WIDE), BF)
    packed = pl.pallas_call(
        pack_kernel,
        out_shape=(pltpu.HBM((rows, WIDE), BF),) * 8,
        in_specs=[smem()] + [vmem()] * 4,
        out_specs=(vmem(),) * 8,
        compiler_params=pltpu.CompilerParams(vmem_limit_bytes=8 * MIB),
        name="pack",
    )(info, queries, out_grad, keys, values)
    pieces, packed = lax.optimization_barrier((pieces, packed))
    inner = pl.pallas_call(
        select_kernel,
        out_shape=jax.ShapeDtypeStruct((CHIPS, INNER * 32, HD), BF),
        in_specs=[smem(), vmem()],
        out_specs=vmem(),
        compiler_params=pltpu.CompilerParams(vmem_limit_bytes=6 * MIB),
        name="select_inner",
    )(info, pieces.reshape(NODES, 32, HD))
    far = lax.all_to_all(inner, "chip", split_axis=0, concat_axis=0, tiled=True)
    arrived = exchange(packed[:5], PIECES[:5])
    later, arrived[1] = lax.optimization_barrier((packed[5:], arrived[1]))
    arrived += exchange(later, PIECES[5:])

    half = jax.ShapeDtypeStruct((4 * SEG, HD), F32)

    def attend(dc, operands):
        last = dc == 1
        out_shape = (piece_shape,) * 4
        out_specs = (vmem(),) * 4
        scratch_shapes = [
            pltpu.VMEM((SEG, WIDE), BF),
            pltpu.VMEM((SEG, WIDE), BF),
            pltpu.VMEM((4 * SEG, HD), BF),
            pltpu.VMEM((4 * SEG, HD), BF),
            pltpu.VMEM((SEG, 4 * SEG), F32),
            pltpu.VMEM((GROUP * SEG, 4 * SEG), BF),
            pltpu.VMEM((GROUP * SEG, 4 * SEG), BF),
        ]
        if last:
            out_shape += (jax.ShapeDtypeStruct((CHIPS, INNER * 32, HD), BF),)
            out_specs += (vmem(),)
            scratch_shapes.append(pltpu.VMEM((CHIPS, INNER * 32, HD), F32))
        else:
            out_shape += (half, half)
            out_specs += (vmem(), vmem())
        return pl.pallas_call(
            functools.partial(attention_kernel, dc),
            out_shape=out_shape,
            in_specs=[smem()] + [vmem()] * (7 if last else 5),
            out_specs=out_specs,
            scratch_shapes=scratch_shapes,
            compiler_params=pltpu.CompilerParams(vmem_limit_bytes=20 * MIB),
            cost_estimate=pl.CostEstimate(
                flops=2 * 5 * GROUP * SEG * 4 * SEG * HD * 4,
                bytes_accessed=6 * 1024 * 1024,
                transcendentals=GROUP * SEG * 4 * SEG,
            ),
            name="attention",
        )(info, far, *operands)

    *leaving, first_key, first_value = attend(0, arrived[:4])
    *others, terms = attend(1, arrived[4:] + [first_key, first_value])
    first_back = exchange(leaving, PIECES[:4])
    terms, first_back = lax.optimization_barrier((terms, first_back))

    parts = lax.all_to_all(terms, "chip", split_axis=0, concat_axis=0, tiled=True)
    far_back = exchange(others[1:], PIECES[5:])
    back = first_back + exchange(others[:1], PIECES[4:5]) + far_back
    parts, back = lax.optimization_barrier((parts, back))
    sums = pl.pallas_call(
        sum_kernel,
        out_shape=jax.ShapeDtypeStruct((NODES, 32, HD), BF),
        in_specs=[smem(), vmem()],
        out_specs=vmem(),
        compiler_params=pltpu.CompilerParams(vmem_limit_bytes=6 * MIB),
        name="sum_terms",
    )(info, parts)
    sums = sums.reshape(CHIPS * KV_HEADS, 8, HD)
    sums = lax.all_to_all(sums, ALL, split_axis=0, concat_axis=0, tiled=True)

    wide_shape = jax.ShapeDtypeStruct((rows, KV_HEADS * QW), BF)
    narrow_shape = jax.ShapeDtypeStruct((rows, KV_HEADS * HD), BF)
    attended, query_grad, own_key, own_value = pl.pallas_call(
        unpack_kernel,
        out_shape=(wide_shape, wide_shape, narrow_shape, narrow_shape),
        in_specs=[smem()] + [vmem()] * 8,
        out_specs=(vmem(),) * 4,
        compiler_params=pltpu.CompilerParams(vmem_limit_bytes=8 * MIB),
        name="unpack",
    )(info, *back)
    sums, attended, query_grad, own_key, own_value = lax.optimization_barrier(
        (sums, attended, query_grad, own_key, own_value)
    )
    sums = sums.reshape(2, 8, KV_HEADS, 8, HD).transpose(0, 1, 3, 2, 4)
    sums = sums.reshape(2, rows, KV_HEADS * HD)
    is_inner = node_of_slot[2 * chip + core] < INNER
    key_grad = jnp.where(is_inner, sums[0], own_key)
    value_grad = jnp.where(is_inner, sums[1], own_value)
    return attended, query_grad, key_grad, value_grad


def solution(mesh):
    devices = mesh.devices.reshape(CHIPS, 2, 4)
    inner_mesh = Mesh(devices, ALL)
    split = P(ALL, None)
    return jax.shard_map(
        on_device,
        mesh=inner_mesh,
        in_specs=(split, split, split, split, P(), P(), P()),
        out_specs=(split, split, split, split),
        check_vma=False,
    )
```

```python
import functools

import jax
import jax.numpy as jnp
from jax import lax
from jax.experimental import pallas as pl
from jax.experimental.pallas import tpu as pltpu
from jax.sharding import Mesh
from jax.sharding import PartitionSpec as P

HD = 128
TILE = 128
SEG = 256
GROUP = 5
KV_HEADS = 8
INNER = 8
NODES = 32
CHIPS = 16
QW = GROUP * HD
WIDE = 2 * QW + 2 * HD
SCALE = HD ** (-0.5)
BF = jnp.bfloat16
F32 = jnp.float32
MIB = 1024 * 1024

PARENT, NODE_OF_SLOT, LIVE_TILES, SLOT_OF_NODE, PLACE = 0, 32, 64, 96, 128
INFO_SIZE = 131

ALL = ("chip", "core", "head")
GROUP_AXES = ("core", "head")


def smem():
    return pl.BlockSpec(memory_space=pltpu.SMEM)


def vmem():
    return pl.BlockSpec(memory_space=pltpu.VMEM)


def hbm():
    return pl.BlockSpec(memory_space=pltpu.HBM)


def nt_dot(left, right):
    return lax.dot_general(left, right, (((1,), (1,)), ((), ())), preferred_element_type=F32)


def nn_dot(left, right):
    return lax.dot_general(left, right, (((1,), (0,)), ((), ())), preferred_element_type=F32)


def info_kernel(parent, node_of_slot, live_tiles, info):
    for n in range(NODES):
        info[PARENT + n] = parent[n]
        info[NODE_OF_SLOT + n] = node_of_slot[n]
        info[LIVE_TILES + n] = live_tiles[n]
    for slot in range(NODES):
        info[SLOT_OF_NODE + node_of_slot[slot]] = slot
    for n, axis in enumerate(ALL):
        info[PLACE + n] = lax.axis_index(axis)


def select_kernel(info, pieces, out):
    for node in range(INNER):
        block = pieces[info[SLOT_OF_NODE + node]]
        for chip in range(CHIPS):
            out[chip, node * 32 : node * 32 + 32, :] = block


SHIFTS = (0, 2, 1, 3)
PIECES = [(dc, dx) for dc in range(2) for dx in SHIFTS]


def group_index(info, dc, dx):
    return lax.rem(info[PLACE + 1] + dc, 2) * 4 + lax.rem(info[PLACE + 2] + dx, 4)


def pack_kernel(info, queries, out_grad, keys, values, *outs):
    for (dc, dx), out in zip(PIECES, outs):
        peer = group_index(info, dc, dx)
        wide = pl.ds(pl.multiple_of(peer * QW, HD), QW)
        narrow = pl.ds(pl.multiple_of(peer * HD, HD), HD)
        out[:, 0:QW] = queries[:, wide]
        out[:, QW : 2 * QW] = out_grad[:, wide]
        out[:, 2 * QW : 2 * QW + HD] = keys[:, narrow]
        out[:, 2 * QW + HD : WIDE] = values[:, narrow]


def unpack_kernel(info, *refs):
    pieces, (attended, query_grad, own_key, own_value) = refs[:8], refs[8:]
    for (dc, dx), piece in zip(PIECES, pieces):
        peer = group_index(info, 2 - dc, 4 - dx)
        wide = pl.ds(pl.multiple_of(peer * QW, HD), QW)
        narrow = pl.ds(pl.multiple_of(peer * HD, HD), HD)
        attended[:, wide] = piece[:, 0:QW]
        query_grad[:, wide] = piece[:, QW : 2 * QW]
        own_key[:, narrow] = piece[:, 2 * QW : 2 * QW + HD]
        own_value[:, narrow] = piece[:, 2 * QW + HD : WIDE]


def exchange(pieces, shifts):
    moved = []
    for (dc, dx), piece in zip(shifts, pieces):
        if dc or dx:
            pairs = [
                (4 * c + x, 4 * ((c + dc) % 2) + (x + dx) % 4) for c in range(2) for x in range(4)
            ]
            piece = lax.ppermute(piece, GROUP_AXES, pairs)
        moved.append(piece)
    return moved


def attention_kernel(dc, info, far, *refs):
    arrived, refs = refs[:4], refs[4:]
    if dc == 0:
        leaving, key_out, value_out, refs = refs[:4], refs[4], refs[5], refs[6:]
    else:
        first_key, first_value, leaving, terms, refs = refs[0], refs[1], refs[2:6], refs[6], refs[7:]
    mine, out, key_all, value_all, bias, probs_all, dscores_all = refs[:7]
    quarters = [
        pl.ds(pl.multiple_of(lax.rem(info[PLACE + 2] + 4 - dx, 4) * 64, 64), 64) for dx in SHIFTS
    ]
    for quarter, piece in zip(quarters, arrived):
        mine[quarter, :] = piece[...]
    row = lax.broadcasted_iota(jnp.int32, (SEG, SEG), 0)
    token = lax.broadcasted_iota(jnp.int32, (SEG, SEG), 1)
    bias[:, 0:SEG] = jnp.where(token <= row, 0.0, -jnp.inf)
    tile = (token >> 4) & 1

    def lineage(which):
        me = info[NODE_OF_SLOT + 2 * info[PLACE] + lax.rem(info[PLACE + 1] + which, 2)]
        chain = [me]
        for _ in range(3):
            current = chain[-1]
            chain.append(jnp.where(current >= 0, info[PARENT + jnp.maximum(current, 0)], -1))
        return chain

    def accumulate(chain, part, first):
        for step in range(1, 4):
            rows = pl.ds(pl.multiple_of(jnp.maximum(chain[step], 0) * 32, 32), 32)
            here = slice(step * SEG, (step + 1) * SEG)
            acc[first : first + 8, rows, :] += part[here].reshape(8, 32, HD)
        rows = pl.ds(pl.multiple_of(jnp.minimum(chain[0], INNER) * 32, 32), 32)
        own = part[0:SEG].reshape(4, 8, 8, HD)
        for piece in range(8):
            acc[first + piece, rows, :] += own[:, piece].reshape(32, HD)

    if dc == 1:
        acc = refs[7]
        acc[...] = jnp.zeros_like(acc)
        accumulate(lineage(0), first_key[...], 0)
        accumulate(lineage(0), first_value[...], 8)

    for step, node in enumerate(lineage(dc)[1:], 1):
        safe = jnp.maximum(node, 0)
        live = jnp.where(node >= 0, info[LIVE_TILES + safe], 0)
        rows = pl.ds(pl.multiple_of(safe * 32, 32), 32)
        here = slice(step * SEG, (step + 1) * SEG)
        key_all[here, :] = far[0:8, rows, :].reshape(SEG, HD)
        value_all[here, :] = far[8:16, rows, :].reshape(SEG, HD)
        bias[:, here] = jnp.where(tile < live, 0.0, -jnp.inf)
    key_all[0:SEG, :] = mine[:, 2 * QW : 2 * QW + HD]
    value_all[0:SEG, :] = mine[:, 2 * QW + HD : WIDE]

    keys = key_all[...]
    values = value_all[...]
    queries_t = []
    grads_t = []
    for g in range(GROUP):
        columns = slice(g * HD, (g + 1) * HD)
        grad_columns = slice(QW + g * HD, QW + (g + 1) * HD)
        query = mine[:, columns]
        grad = mine[:, grad_columns]
        queries_t.append(query.T)
        grads_t.append(grad.T)
        scores = nt_dot(query, keys) * SCALE + bias[...]
        peak = jnp.max(scores, axis=1, keepdims=True)
        weight = jnp.exp(scores - peak)
        total = jnp.sum(weight, axis=1, keepdims=True)
        probs = weight * jnp.exp(peak - (peak + jnp.log(total)))
        probs_b = probs.astype(BF)
        attended = nn_dot(probs_b, values).astype(BF)
        out[:, columns] = attended
        delta = jnp.sum(grad.astype(F32) * attended.astype(F32), axis=1, keepdims=True)
        dprobs = nt_dot(grad, values)
        dscores = (probs * (dprobs - delta)).astype(BF)
        query_grad = nn_dot(dscores, keys) * SCALE
        out[:, grad_columns] = query_grad.astype(BF)
        probs_all[g * SEG : (g + 1) * SEG, :] = probs_b
        dscores_all[g * SEG : (g + 1) * SEG, :] = dscores
    value_terms = nn_dot(jnp.concatenate(grads_t, 1), probs_all[...]).T
    key_terms = nn_dot(jnp.concatenate(queries_t, 1), dscores_all[...]).T * SCALE
    out[:, 2 * QW : 2 * QW + HD] = key_terms[0:SEG].astype(BF)
    out[:, 2 * QW + HD : WIDE] = value_terms[0:SEG].astype(BF)
    quarters = [
        pl.ds(pl.multiple_of(lax.rem(info[PLACE + 2] + dx, 4) * 64, 64), 64) for dx in SHIFTS
    ]
    for quarter, piece in zip(quarters, leaving):
        piece[...] = out[quarter, :]

    if dc == 0:
        key_out[...] = key_terms
        value_out[...] = value_terms
    else:
        accumulate(lineage(1), value_terms, 8)
        accumulate(lineage(1), key_terms, 0)
        terms[...] = acc[:, 0 : INNER * 32, :].astype(BF)


def sum_kernel(info, parts, out):
    out[...] = jnp.zeros_like(out)
    for node in range(INNER):
        rows = slice(node * 32, node * 32 + 32)
        sums = parts[0, rows, :].astype(F32)
        for chip in range(1, CHIPS):
            sums = sums + parts[chip, rows, :].astype(F32)
        out[info[SLOT_OF_NODE + node]] = sums.astype(BF)


def on_device(queries, keys, values, out_grad, parent, node_of_slot, live_tiles):
    rows = queries.shape[0]
    chip = lax.axis_index("chip")
    core = lax.axis_index("core")
    info = pl.pallas_call(
        info_kernel,
        out_shape=pltpu.SMEM((INFO_SIZE,), jnp.int32),
        in_specs=[smem()] * 3,
        out_specs=smem(),
        name="info",
    )(parent, node_of_slot, live_tiles)

    pieces = jnp.concatenate([keys, values], 0).reshape(16, 8, KV_HEADS, HD)
    pieces = pieces.transpose(0, 2, 1, 3).reshape(CHIPS * KV_HEADS, 8, HD)
    pieces = lax.all_to_all(pieces, ALL, split_axis=0, concat_axis=0, tiled=True)
    piece_shape = jax.ShapeDtypeStruct((rows, WIDE), BF)
    packed = pl.pallas_call(
        pack_kernel,
        out_shape=(pltpu.HBM((rows, WIDE), BF),) * 8,
        in_specs=[smem()] + [vmem()] * 4,
        out_specs=(vmem(),) * 8,
        compiler_params=pltpu.CompilerParams(vmem_limit_bytes=8 * MIB),
        name="pack",
    )(info, queries, out_grad, keys, values)
    pieces, packed = lax.optimization_barrier((pieces, packed))
    inner = pl.pallas_call(
        select_kernel,
        out_shape=jax.ShapeDtypeStruct((CHIPS, INNER * 32, HD), BF),
        in_specs=[smem(), vmem()],
        out_specs=vmem(),
        compiler_params=pltpu.CompilerParams(vmem_limit_bytes=6 * MIB),
        name="select_inner",
    )(info, pieces.reshape(NODES, 32, HD))
    far = lax.all_to_all(inner, "chip", split_axis=0, concat_axis=0, tiled=True)
    arrived = exchange(packed[:5], PIECES[:5])
    later, arrived[1] = lax.optimization_barrier((packed[5:], arrived[1]))
    arrived += exchange(later, PIECES[5:])

    half = jax.ShapeDtypeStruct((4 * SEG, HD), F32)

    def attend(dc, operands):
        last = dc == 1
        out_shape = (piece_shape,) * 4
        out_specs = (vmem(),) * 4
        scratch_shapes = [
            pltpu.VMEM((SEG, WIDE), BF),
            pltpu.VMEM((SEG, WIDE), BF),
            pltpu.VMEM((4 * SEG, HD), BF),
            pltpu.VMEM((4 * SEG, HD), BF),
            pltpu.VMEM((SEG, 4 * SEG), F32),
            pltpu.VMEM((GROUP * SEG, 4 * SEG), BF),
            pltpu.VMEM((GROUP * SEG, 4 * SEG), BF),
        ]
        if last:
            out_shape += (jax.ShapeDtypeStruct((CHIPS, INNER * 32, HD), BF),)
            out_specs += (vmem(),)
            scratch_shapes.append(pltpu.VMEM((CHIPS, (INNER + 1) * 32, HD), F32))
        else:
            out_shape += (half, half)
            out_specs += (vmem(), vmem())
        return pl.pallas_call(
            functools.partial(attention_kernel, dc),
            out_shape=out_shape,
            in_specs=[smem()] + [vmem()] * (7 if last else 5),
            out_specs=out_specs,
            scratch_shapes=scratch_shapes,
            compiler_params=pltpu.CompilerParams(vmem_limit_bytes=20 * MIB),
            cost_estimate=pl.CostEstimate(
                flops=2 * 5 * GROUP * SEG * 4 * SEG * HD * 4,
                bytes_accessed=6 * 1024 * 1024,
                transcendentals=GROUP * SEG * 4 * SEG,
            ),
            name="attention",
        )(info, far, *operands)

    *leaving, first_key, first_value = attend(0, arrived[:4])
    *others, terms = attend(1, arrived[4:] + [first_key, first_value])
    first_back = exchange(leaving, PIECES[:4])
    terms, first_back = lax.optimization_barrier((terms, first_back))

    parts = lax.all_to_all(terms, "chip", split_axis=0, concat_axis=0, tiled=True)
    far_back = exchange(others[1:], PIECES[5:])
    back = first_back + exchange(others[:1], PIECES[4:5]) + far_back
    parts, back = lax.optimization_barrier((parts, back))
    sums = pl.pallas_call(
        sum_kernel,
        out_shape=jax.ShapeDtypeStruct((NODES, 32, HD), BF),
        in_specs=[smem(), vmem()],
        out_specs=vmem(),
        compiler_params=pltpu.CompilerParams(vmem_limit_bytes=6 * MIB),
        name="sum_terms",
    )(info, parts)
    sums = sums.reshape(CHIPS * KV_HEADS, 8, HD)
    sums = lax.all_to_all(sums, ALL, split_axis=0, concat_axis=0, tiled=True)

    wide_shape = jax.ShapeDtypeStruct((rows, KV_HEADS * QW), BF)
    narrow_shape = jax.ShapeDtypeStruct((rows, KV_HEADS * HD), BF)
    attended, query_grad, own_key, own_value = pl.pallas_call(
        unpack_kernel,
        out_shape=(wide_shape, wide_shape, narrow_shape, narrow_shape),
        in_specs=[smem()] + [vmem()] * 8,
        out_specs=(vmem(),) * 4,
        compiler_params=pltpu.CompilerParams(vmem_limit_bytes=8 * MIB),
        name="unpack",
    )(info, *back)
    sums, attended, query_grad, own_key, own_value = lax.optimization_barrier(
        (sums, attended, query_grad, own_key, own_value)
    )
    sums = sums.reshape(2, 8, KV_HEADS, 8, HD).transpose(0, 1, 3, 2, 4)
    sums = sums.reshape(2, rows, KV_HEADS * HD)
    is_inner = node_of_slot[2 * chip + core] < INNER
    key_grad = jnp.where(is_inner, sums[0], own_key)
    value_grad = jnp.where(is_inner, sums[1], own_value)
    return attended, query_grad, key_grad, value_grad


def solution(mesh):
    devices = mesh.devices.reshape(CHIPS, 2, 4)
    inner_mesh = Mesh(devices, ALL)
    split = P(ALL, None)
    return jax.shard_map(
        on_device,
        mesh=inner_mesh,
        in_specs=(split, split, split, split, P(), P(), P()),
        out_specs=(split, split, split, split),
        check_vma=False,
    )
```
